512 devices in a mesh: fsdp: 128 (over y, z, core), tp: 4 (over x).
Axes of the slice: x: 4, y: 4, z: 16, core: 2. Of those that a mesh axis runs over, the one named last changes fastest.
Arguments:
- grads: bfloat16 [16, 512, 16, 512], P(None, 'fsdp', None, 'tp'), may hold values from -1.5 to 1.5
- second_moment: bfloat16 [16, 512, 16, 512], P(None, 'fsdp', None, 'tp'), may hold values from 0.0009994507 to 0.099609375
- owner: int32 [16, 16], replicated, may hold values from 0 to 127, as said below
- left_factor: bfloat16 [640, 512, 512], P('fsdp', 'tp'), may hold values from -1 to 11
- right_factor: bfloat16 [640, 512, 512], P('fsdp', 'tp'), may hold values from -1 to 11
- left_root: bfloat16 [640, 512, 512], P('fsdp', 'tp'), may hold values from -0.2 to 1.2
- right_root: bfloat16 [640, 512, 512], P('fsdp', None, 'tp'), may hold values from -0.2 to 1.2
Outputs:
- update: bfloat16 [16, 512, 16, 512], P(None, 'fsdp', None, 'tp')
- moment_new: bfloat16 [16, 512, 16, 512], P(None, 'fsdp', None, 'tp')
- left_new: bfloat16 [640, 512, 512], P('fsdp', 'tp')
- right_new: bfloat16 [640, 512, 512], P('fsdp', 'tp')
The draws below stay inside these ranges and needn't reach their ends.
Inputs may be any that keep to these rules, and one draw needn't show every extreme that they name: No owner holds more than 5 blocks and some owner holds exactly 5; no owner holds more than 2 blocks of one block row and some owner holds exactly 2; the 4 consecutive owners starting at some owner hold none.
All inputs are finite; a program needn't handle non-finite values.
Results may differ from the reference program's by a relative error of at most 0.0057.
Values may be sent and summed in bfloat16 or wider, within the bound.
A program may use at most 64 MiB of HBM per device.

```python
import math
import jax
import jax.numpy as jnp
from jax import lax

B = 512
ROW_DEV = 64
CAP = 5
D = 8192
NBR = 16
NBC = 16
SLOTS = 640
LOST = 4


def square_block(noise, diag_key, low_exp, high_exp):
    scales = 10.0 ** jax.random.uniform(diag_key, (SLOTS, B), minval=low_exp, maxval=high_exp)
    return noise + scales[:, :, None] * jnp.eye(B, dtype=jnp.float32)[None]


def draw_grads(key, part):
    key = jax.random.fold_in(key, 3)
    noise_key, row_key = jax.random.split(key, 2)
    row_scale = 0.02 * 10.0 ** jax.random.uniform(row_key, (NBR, B, 1, 1))
    values = row_scale * jnp.clip(jax.random.normal(noise_key, (NBR, B, NBC, B)), -6.0, 6.0)
    return values.astype(jnp.bfloat16)


def draw_owner(key, part):
    key = jax.random.fold_in(key, 5)
    shift_key, start_key, hop_key = jax.random.split(key, 3)
    owner_total = D // ROW_DEV
    spacing = max(NBR // 2, 1)
    shifts = jax.random.randint(shift_key, (NBR, 1), 0, NBC)
    start = jax.random.randint(start_key, (), 0, owner_total)
    hop = jax.random.randint(hop_key, (), 1, max(owner_total // spacing, 2))
    row_ids = jnp.arange(NBR)[:, None]
    col_ids = jnp.arange(NBC)[None, :]
    position = (col_ids + shifts) % NBC * NBR + row_ids
    virtual = position // 2
    offset = (virtual - start) % owner_total

    def receiver(index):
        return (start + index + spacing * hop) % owner_total
    first = jnp.where(offset == 1, receiver(0), receiver(offset))
    moved = jnp.where(position % 2 == 0, first, receiver(offset))
    return jnp.where(offset < LOST, moved, virtual).astype(jnp.int32)


def draw_left_factor(key, part):
    key = jax.random.fold_in(key, 11)
    noise_key, diag_key = jax.random.split(key)
    noise = 0.1 * jnp.clip(jax.random.normal(noise_key, (SLOTS, B, B)), -6.0, 6.0)
    return square_block(noise, diag_key, 0.0, 1.0).astype(jnp.bfloat16)


def draw_right_factor(key, part):
    key = jax.random.fold_in(key, 12)
    noise_key, diag_key = jax.random.split(key)
    noise = 0.1 * jnp.clip(jax.random.normal(noise_key, (SLOTS, B, B)), -6.0, 6.0)
    return square_block(noise, diag_key, 0.0, 1.0).astype(jnp.bfloat16)


def draw_left_root(key, part):
    key = jax.random.fold_in(key, 13)
    noise_key, diag_key = jax.random.split(key)
    noise = 0.02 * jnp.clip(jax.random.normal(noise_key, (SLOTS, B, B)), -6.0, 6.0)
    return square_block(noise, diag_key, -0.5, 0.0).astype(jnp.bfloat16)


def draw_right_root(key, part):
    key = jax.random.fold_in(key, 14)
    noise_key, diag_key = jax.random.split(key)
    noise = 0.02 * jnp.clip(jax.random.normal(noise_key, (SLOTS, B, B)), -6.0, 6.0)
    return square_block(noise, diag_key, -0.5, 0.0).astype(jnp.bfloat16)


def levels(own_key, dims, cuts, smallest, largest):
    level, own = 1.0, jax.random.fold_in(own_key, 6)
    for axis_at, shards_of in cuts:
        steps = jnp.exp(jax.random.uniform(jax.random.fold_in(own, axis_at), (shards_of,), jnp.float32, smallest / len(cuts), largest / len(cuts)))
        level = level * jnp.repeat(steps, dims[axis_at] // shards_of).reshape([-1 if axis == axis_at else 1 for axis in range(len(dims))])
    return level


def setup_inputs(seed: int = 0) -> dict:
    seeds = jax.random.split(jax.random.key(seed), 8)
    return {
        "grads": draw_grads(jax.random.fold_in(seeds[7], 71), 0),
        "second_moment": jnp.clip(jnp.exp(math.log(0.099609375) - 4.6018058 * jax.random.uniform(seeds[1], (NBR, B, NBC, B), jnp.float32) ** levels(seeds[1], (NBR, B, NBC, B), ((1, 128), (3, 4)), -0.2, 0.2)), 0.0009994507, 0.099609375).astype(jnp.bfloat16),
        "owner": draw_owner(jax.random.fold_in(seeds[7], 71), 0),
        "left_factor": draw_left_factor(jax.random.fold_in(seeds[7], 71), 0),
        "right_factor": draw_right_factor(jax.random.fold_in(seeds[7], 71), 0),
        "left_root": draw_left_root(jax.random.fold_in(seeds[7], 71), 0),
        "right_root": draw_right_root(jax.random.fold_in(seeds[7], 71), 0),
    }


def reference(grads, second_moment, owner, left_factor, right_factor, left_root, right_root):
    flat_owner = owner.reshape(-1).astype(jnp.int32)
    total = flat_owner.shape[0]
    order = jnp.arange(total)
    same = flat_owner[:, None] == flat_owner[None, :]
    slot_rank = lax.optimization_barrier(jnp.sum((same & (order[None, :] < order[:, None])).astype(jnp.int32), axis=1))
    slot_of = (flat_owner * CAP + slot_rank).astype(jnp.int32)
    blocks = grads.transpose(0, 2, 1, 3).reshape(total, B, B)

    def per_block(inputs):
        block_grad, slot = inputs
        gram_left = jnp.dot(block_grad, block_grad.T, preferred_element_type=jnp.float32)
        left_next = (0.9 * left_factor[slot].astype(jnp.float32) + 0.1 * gram_left).astype(jnp.bfloat16)
        gram_right = jnp.dot(block_grad.T, block_grad, preferred_element_type=jnp.float32)
        right_next = (0.9 * right_factor[slot].astype(jnp.float32) + 0.1 * gram_right).astype(jnp.bfloat16)
        rotated = jnp.dot(left_root[slot], block_grad, preferred_element_type=jnp.float32).astype(jnp.bfloat16)
        precond = jnp.dot(rotated, right_root[slot], preferred_element_type=jnp.float32).astype(jnp.bfloat16)
        return (left_next, right_next, precond)
    left_blocks, right_blocks, precond_blocks = lax.map(per_block, (blocks, slot_of))
    left_new = (0.9 * left_factor.astype(jnp.float32) + 0.1 * jnp.zeros((), jnp.float32)).astype(jnp.bfloat16)
    left_new = left_new.at[slot_of].set(left_blocks)
    right_new = (0.9 * right_factor.astype(jnp.float32) + 0.1 * jnp.zeros((), jnp.float32)).astype(jnp.bfloat16)
    right_new = right_new.at[slot_of].set(right_blocks)
    precond_float = precond_blocks.astype(jnp.float32).reshape(NBR, NBC, B, B).transpose(0, 2, 1, 3)
    grad_float = grads.astype(jnp.float32)
    moment = 0.95 * second_moment.astype(jnp.float32) + 0.05 * grad_float * grad_float
    adam = grad_float / (jnp.sqrt(moment) + 1e-08)
    adam_norm = jnp.sqrt(lax.optimization_barrier(jnp.sum(adam * adam, axis=(1, 3))))
    precond_norm = jnp.sqrt(lax.optimization_barrier(jnp.sum(precond_float * precond_float, axis=(1, 3))))
    scale = adam_norm / (precond_norm + 1e-06)
    update = (precond_float * scale[:, None, :, None]).astype(jnp.bfloat16)
    return (update, moment.astype(jnp.bfloat16), left_new, right_new)
```

```python
import functools
import types

import jax
import jax.numpy as jnp
from jax import lax
from jax.experimental import pallas as pl
from jax.experimental.pallas import tpu as pltpu
from jax.sharding import PartitionSpec as P

BF, F32, I32 = jnp.bfloat16, jnp.float32, jnp.int32
MESH = pl.DeviceIdType.MESH
CAP = 5
MAIN = 2
REST = CAP - MAIN
LANES = 128


def cfg_of(NY, NZ, NC, NX, R, Q, NBR, NBC, CB, cid):
    c = types.SimpleNamespace(NY=NY, NZ=NZ, NC=NC, NX=NX, R=R, Q=Q, NBR=NBR, NBC=NBC, CB=CB, cid=cid)
    c.NG = NY * NC
    c.NB = NBR * NBC
    c.B = NX * Q
    c.W = R * Q
    assert c.B == NY * NZ * NC * R
    return c


def idiv(x, d):
    if d & (d - 1) == 0:
        return lax.shift_right_logical(x, jnp.int32(d.bit_length() - 1))
    return lax.shift_right_logical(x * jnp.int32(-(-(1 << 16) // d)), jnp.int32(16))


def imod(x, d):
    if d & (d - 1) == 0:
        return x & jnp.int32(d - 1)
    return x - idiv(x, d) * jnp.int32(d)


def iota(shape, dim):
    return lax.broadcasted_iota(I32, shape, dim)


def hot(cond):
    return jnp.where(cond, 1.0, 0.0).astype(BF)


def dot(a, b):
    return jnp.dot(a, b, preferred_element_type=F32)


def scratch_of(c):
    vm = lambda *s: pltpu.VMEM(s, BF)
    vf = lambda *s: pltpu.VMEM(s, F32)
    dma = lambda *s: pltpu.SemaphoreType.DMA(s)
    out = {}
    for name in ("sA", "rA", "sI", "rI"):
        out[name] = vm(c.NZ, MAIN * c.NG, c.W)
    for name in ("sB", "rB", "sJ", "rJ"):
        out[name] = vm(c.NZ, c.R * c.CB, c.Q)
    for name in ("sC", "rC", "sF", "rF"):
        out[name] = vm(c.NG, MAIN, c.NZ, c.W)
    for name in ("sE", "rE", "sH", "rH"):
        out[name] = vm(c.NG, REST, c.NZ, c.W)
    out["gown"] = vm(CAP, c.B, c.Q)
    out["gfull"] = vm(CAP, c.B, c.B)
    out["lfull"] = vm(CAP, c.B, c.B)
    out["rv"] = vm(CAP, c.B, c.Q)
    for name in ("lfv", "rfv", "lnv", "rnv"):
        out[name] = vm(CAP, c.Q, c.B)
    out["pre"] = vf(CAP, c.B, c.Q)
    out["pi"] = vm(c.B, c.B)
    out["pit"] = vm(c.B, c.B)
    out["az"] = vf(c.NZ, 1, LANES)
    out["azr"] = vf(c.NZ, 1, LANES)
    out["ag"] = vf(1, 1, LANES)
    out["agr"] = vf(c.NG, 1, LANES)
    for name in ("ax", "pa", "pb"):
        out[name] = vf(1, 1, LANES)
        out[name + "r"] = vf(c.NX, 1, LANES)
    for name in ("A", "B", "I", "J", "z"):
        out["s_" + name], out["r_" + name] = dma(c.NZ), dma(c.NZ)
    for name in ("C", "E", "F", "H", "g"):
        out["s_" + name], out["r_" + name] = dma(c.NG), dma(c.NG)
    for name in ("x", "pa", "pb"):
        out["s_" + name], out["r_" + name] = dma(c.NX), dma(c.NX)
    for name in ("L1", "L2", "G1", "G2"):
        out["s_" + name], out["r_" + name] = dma(CAP, 2), dma(CAP, 2)
    for name in ("l_lf", "l_rf", "l_rv", "l_lr", "l_ln", "l_rn"):
        out[name] = dma(CAP)
    return out


def kernel(c, names, grads, sm, owner, lf, rf, lr, rr, upd, mom, ln, rn, *scratch):
    w = types.SimpleNamespace(**dict(zip(names, scratch)))
    NZ, NG, NX, NB, R, Q, B, W, CB = c.NZ, c.NG, c.NX, c.NB, c.R, c.Q, c.B, c.W, c.CB
    f = lax.axis_index("fsdp")
    t = lax.axis_index("tp")
    me_c = lax.rem(f, c.NC)
    me_z = lax.rem(lax.div(f, c.NC), NZ)
    me_y = lax.div(f, c.NC * NZ)
    me_g = me_y * c.NC + me_c
    right, left = lax.rem(t + 1, NX), lax.rem(t + NX - 1, NX)

    def at_z(z):
        return {"fsdp": (me_y * NZ + z) * c.NC + me_c, "tp": t}

    def at_g(g):
        return {"fsdp": (lax.div(g, c.NC) * NZ + me_z) * c.NC + lax.rem(g, c.NC), "tp": t}

    def at_x(x):
        return {"fsdp": f, "tp": x}

    def rcopy(src, dst, ssem, rsem, dev):
        return pltpu.make_async_remote_copy(
            src_ref=src, dst_ref=dst, send_sem=ssem, recv_sem=rsem, device_id=dev, device_id_type=MESH
        )

    def loop(lo, hi, body):
        def step(k, carry):
            body(k)
            return carry
        lax.fori_loop(lo, hi, step, 0)

    def each_z(body):
        half = NZ // 2
        body(lax.rem(me_z + half, NZ))
        if half > 1:
            def pair(k):
                d = half - 1 - k
                body(lax.rem(me_z + d, NZ))
                body(lax.rem(me_z + NZ - d, NZ))
            loop(0, half - 1, pair)

    def each_g(body):
        loop(1, NG, lambda k: body(lax.rem(me_g + k, NG)))

    def each_x(body):
        loop(1, NX, lambda k: body(lax.rem(t + k, NX)))

    class Exchange:
        def __init__(self, each, at, me, src, dst, sems):
            self.each, self.at, self.me, self.src, self.dst = each, at, me, src, dst
            self.ss, self.rs = getattr(w, "s_" + sems), getattr(w, "r_" + sems)

        def start(self):
            def go(p):
                rcopy(self.src(p), self.dst.at[self.me], self.ss.at[p], self.rs.at[self.me], self.at(p)).start()
            self.each(go)

        def recv(self):
            def go(p):
                rcopy(self.src(p), self.dst.at[p], self.ss.at[p], self.rs.at[p], self.at(p)).wait_recv()
            self.each(go)

        def sent(self):
            def go(p):
                rcopy(self.src(p), self.dst.at[p], self.ss.at[p], self.rs.at[p], self.at(p)).wait_send()
            self.each(go)

    def one(buf):
        return lambda p: buf.at[0]

    def many(buf):
        return lambda p: buf.at[p]

    xA = Exchange(each_z, at_z, me_z, many(w.sA), w.rA, "A")
    xB = Exchange(each_z, at_z, me_z, many(w.sB), w.rB, "B")
    xI = Exchange(each_z, at_z, me_z, many(w.sI), w.rI, "I")
    xJ = Exchange(each_z, at_z, me_z, many(w.sJ), w.rJ, "J")
    xz = Exchange(each_z, at_z, me_z, many(w.az), w.azr, "z")
    xC = Exchange(each_g, at_g, me_g, many(w.sC), w.rC, "C")
    xE = Exchange(each_g, at_g, me_g, many(w.sE), w.rE, "E")
    xF = Exchange(each_g, at_g, me_g, many(w.sF), w.rF, "F")
    xH = Exchange(each_g, at_g, me_g, many(w.sH), w.rH, "H")
    xg = Exchange(each_g, at_g, me_g, one(w.ag), w.agr, "g")
    xx = Exchange(each_x, at_x, t, one(w.ax), w.axr, "x")
    xpa = Exchange(each_x, at_x, t, one(w.pa), w.par, "pa")
    xpb = Exchange(each_x, at_x, t, one(w.pb), w.pbr, "pb")

    def shard_rows(x):
        return pl.multiple_of(x * Q, Q)

    def l_first(s, d):
        dst = w.lfull.at[s, pl.ds(shard_rows(t), Q), :]
        return rcopy(lr.at[s], dst, w.s_L1.at[s, d], w.r_L1.at[s, d], at_x(right if d == 0 else left))

    def l_pass(s, d):
        x = left if d == 0 else right
        part = w.lfull.at[s, pl.ds(pl.multiple_of(x * Q + d * (Q // 2), Q // 2), Q // 2), :]
        return rcopy(part, part, w.s_L2.at[s, d], w.r_L2.at[s, d], at_x(right if d == 0 else left))

    def g_first(s, d):
        dst = w.gfull.at[s, :, pl.ds(shard_rows(t), Q)]
        return rcopy(w.gown.at[s], dst, w.s_G1.at[s, d], w.r_G1.at[s, d], at_x(right if d == 0 else left))

    def g_pass(s, d):
        x = left if d == 0 else right
        part = w.gfull.at[s, pl.ds(d * (B // 2), B // 2), pl.ds(shard_rows(x), Q)]
        return rcopy(part, part, w.s_G2.at[s, d], w.r_G2.at[s, d], at_x(right if d == 0 else left))

    def pass_on(first, onward, s):
        for d in (0, 1):
            first(s, d).wait_recv()
            onward(s, d).start()

    barrier = pltpu.get_barrier_semaphore()

    def greet(at):
        def go(p):
            pl.semaphore_signal(barrier, inc=1, device_id=at(p), device_id_type=MESH)
        return go
    each_z(greet(at_z))
    each_g(greet(at_g))
    each_x(greet(at_x))

    def local(src, dst, sem):
        return pltpu.make_async_copy(src, dst, sem)

    def l_own(s):
        return local(lr.at[s], w.lfull.at[s, pl.ds(shard_rows(t), Q), :], w.l_lr.at[s])

    def loads(s):
        return (
            local(rr.at[s], w.rv.at[s], w.l_rv.at[s]),
            local(lf.at[s], w.lfv.at[s], w.l_lf.at[s]),
            local(rf.at[s], w.rfv.at[s], w.l_rf.at[s]),
        )

    spread = hot(imod(iota((c.NBC, NB), 1), c.NBC) == iota((c.NBC, NB), 0))
    wide = dot(owner[...].astype(F32).astype(BF), spread)
    own_row = jnp.sum(
        jnp.where(idiv(iota((c.NBR, NB), 1), c.NBC) == iota((c.NBR, NB), 0), wide, 0.0), axis=0, keepdims=True
    )
    i0, i1 = iota((NB, NB), 0), iota((NB, NB), 1)
    own_col = jnp.sum(jnp.where(i0 == i1, own_row, 0.0), axis=1, keepdims=True)
    same = own_row == own_col
    rank_row = jnp.sum(jnp.where(same & (i0 < i1), 1.0, 0.0), axis=0, keepdims=True).astype(I32)
    rank_col = jnp.sum(jnp.where(same & (i1 < i0), 1.0, 0.0), axis=1, keepdims=True).astype(I32)
    own_row, own_col = own_row.astype(I32), own_col.astype(I32)
    key_row, key_col = own_row * 8 + rank_row, own_col * 8 + rank_col
    z_row, z_col = imod(idiv(own_row, c.NC), NZ), imod(idiv(own_col, c.NC), NZ)

    def key_of(z, g, s):
        return ((idiv(g, c.NC) * NZ + z) * c.NC + imod(g, c.NC)) * 8 + s

    def key_main(m):
        return key_of(idiv(m, MAIN * NG), imod(m, NG), imod(idiv(m, NG), MAIN))

    places = NZ * MAIN * NG
    sel_main = hot(key_main(iota((places, 1), 0)) == key_row)
    for r in range(R):
        block = grads[:, r, :, :].reshape(NB, Q)
        w.sA[:, :, r * Q:(r + 1) * Q] = dot(sel_main, block).astype(BF).reshape(NZ, MAIN * NG, Q)

    pl.semaphore_wait(barrier, NZ - 1 + NG - 1 + NX - 1)
    xA.start()
    for s in range(MAIN):
        for d in (0, 1):
            l_first(s, d).start()

    over_row, over_col = rank_row >= MAIN, rank_col >= MAIN
    mates = (z_row == z_col)
    pos_row = jnp.sum(jnp.where(mates & over_col & (i0 < i1), 1.0, 0.0), axis=0, keepdims=True).astype(I32)
    pos_col = jnp.sum(jnp.where(mates & over_row & (i1 < i0), 1.0, 0.0), axis=1, keepdims=True).astype(I32)
    PB = NZ * R * CB
    rest_row = jnp.where(over_row & (pos_row < CB), z_row * CB + pos_row, -1)
    rest_col = jnp.where(over_col & (pos_col < CB), z_col * CB + pos_col, -1)

    def rest_parts(m):
        return idiv(m, R * CB), imod(idiv(m, CB), R), imod(m, CB)

    mz, mr, mb = rest_parts(iota((PB, 1), 0))
    lz, lrr, lb = rest_parts(iota((1, PB), 1))
    m_rest, l_rest = mz * CB + mb, lz * CB + lb
    total = jnp.zeros((PB, Q), F32)
    for r in range(R):
        sel = hot(jnp.where(mr == r, m_rest, -2) == rest_row)
        total += dot(sel, grads[:, r, :, :].reshape(NB, Q))
    w.sB[...] = total.astype(BF).reshape(NZ, R * CB, Q)
    xB.start()
    w.rA[pl.ds(me_z, 1)] = w.sA[pl.ds(me_z, 1)]
    w.rB[pl.ds(me_z, 1)] = w.sB[pl.ds(me_z, 1)]
    for s in range(MAIN, CAP):
        for d in (0, 1):
            l_first(s, d).start()
    for s in range(CAP):
        l_own(s).start()
        for copy in loads(s):
            copy.start()

    adam_col = jnp.zeros((NB, 1), F32)
    for r in range(R):
        g = grads[:, r, :, :].astype(F32)
        moment = 0.95 * sm[:, r, :, :].astype(F32) + 0.05 * g * g
        mom[:, r, :, :] = moment.astype(BF)
        adam = g / (jnp.sqrt(moment) + 1e-08)
        adam_col += jnp.sum((adam * adam).reshape(NB, Q), axis=1, keepdims=True)
    lane = iota((1, LANES), 1)
    lane_key = jnp.where(lane < NG * 8, key_of(jnp.zeros_like(lane), idiv(lane, 8), imod(lane, 8)), -1)

    def sums_for(z):
        hit = (key_col - z * (c.NC * 8)) == lane_key
        w.az[pl.ds(z, 1)] = jnp.sum(jnp.where(hit, adam_col, 0.0), axis=0, keepdims=True)[None]
    loop(0, NZ, sums_for)
    xz.start()
    w.azr[pl.ds(me_z, 1)] = w.az[pl.ds(me_z, 1)]

    def natural(m):
        r, g, z = idiv(m, NG * NZ), imod(idiv(m, NZ), NG), imod(m, NZ)
        return ((idiv(g, c.NC) * NZ + z) * c.NC + imod(g, c.NC)) * R + r
    w.pi[...] = hot(iota((B, B), 0) == natural(iota((1, B), 1)))
    w.pit[...] = hot(natural(iota((B, 1), 0)) == iota((B, B), 1))

    def turned(m):
        return (imod(m, NZ) * MAIN + imod(idiv(m, NZ), MAIN)) * NG + idiv(m, NZ * MAIN)
    to_gsz = hot(turned(iota((places, 1), 0)) == iota((places, places), 1))
    to_zsg = hot(iota((places, places), 0) == turned(iota((1, places), 1)))

    held_row = jnp.sum(
        jnp.where(rest_col == me_z * CB + lb, key_col + 1, 0), axis=0, keepdims=True
    ) - 1
    held_col = jnp.sum(
        jnp.where(me_z * CB + mb == rest_row, key_row + 1, 0), axis=1, keepdims=True
    ) - 1

    def rest_slots(m):
        return idiv(m, REST * NZ), imod(idiv(m, NZ), REST) + MAIN, imod(m, NZ)
    PS = NG * REST * NZ
    ag_, as_, az_ = rest_slots(iota((PS, 1), 0))
    slot_col = key_of(me_z, ag_, as_)
    bg_, bs_, bz_ = rest_slots(iota((1, PS), 1))
    slot_row = key_of(me_z, bg_, bs_)

    for s in range(MAIN):
        pass_on(l_first, l_pass, s)

    xA.recv()
    w.sC[...] = dot(to_gsz, w.rA[...].reshape(places, W)).astype(BF).reshape(NG, MAIN, NZ, W)
    xC.start()
    w.rC[pl.ds(me_g, 1)] = w.sC[pl.ds(me_g, 1)]

    xB.recv()
    flat = w.rB[...].reshape(PB, Q)
    hits = (slot_col == held_row) & (az_ == lz)
    for r in range(R):
        got = dot(hot(hits & (lrr == r)), flat)
        w.sE[:, :, :, r * Q:(r + 1) * Q] = got.astype(BF).reshape(NG, REST, NZ, Q)
    xE.start()
    w.rE[pl.ds(me_g, 1)] = w.sE[pl.ds(me_g, 1)]

    xz.recv()
    w.ag[...] = jnp.sum(w.azr[...], axis=0, keepdims=True)
    xg.start()
    w.agr[pl.ds(me_g, 1)] = w.ag[...]

    for s in range(MAIN, CAP):
        pass_on(l_first, l_pass, s)

    def own_cols(buf, s, at):
        rows = [buf[:, s, :, r * Q:(r + 1) * Q].reshape(NG * NZ, Q) for r in range(R)]
        cols = dot(w.pi[...], jnp.concatenate(rows, axis=0)).astype(BF)
        w.gown[at] = cols
        w.gfull[at, :, pl.ds(shard_rows(t), Q)] = cols
        for d in (0, 1):
            g_first(at, d).start()

    xC.recv()
    for s in range(MAIN):
        own_cols(w.rC, s, s)
    xE.recv()
    for s in range(REST):
        own_cols(w.rE, s, MAIN + s)

    xg.recv()
    w.ax[...] = jnp.sum(w.agr[...], axis=0, keepdims=True)
    xx.start()
    w.axr[pl.ds(t, 1)] = w.ax[...]

    for s in range(MAIN):
        pass_on(g_first, g_pass, s)

    def precond(s):
        l_own(s).wait()
        local(rr.at[s], w.rv.at[s], w.l_rv.at[s]).wait()
        for d in (0, 1):
            l_pass(s, d).wait_recv()
            g_pass(s, d).wait_recv()
        turned_cols = dot(w.gfull[s], w.rv[s]).astype(BF)
        out = dot(w.lfull[s], turned_cols)
        w.pre[s] = out
        return jnp.sum(jnp.sum(out * out, axis=0, keepdims=True), axis=1, keepdims=True)

    def norms(slots, buf):
        row = jnp.zeros((1, LANES), F32)
        for s in slots:
            row = jnp.where(lane == s, precond(s), row)
        buf[...] = row[None]

    norms(range(MAIN), w.pa)
    xpa.start()
    w.par[pl.ds(t, 1)] = w.pa[...]
    for s in range(MAIN, CAP):
        pass_on(g_first, g_pass, s)

    xx.recv()
    adam_all = jnp.sum(w.axr[...], axis=0)

    def scaled(slots, sums, dest):
        pre_all = jnp.sum(sums[...], axis=0)
        for k, s in enumerate(slots):
            adam_sum = jnp.sum(jnp.where(lane == me_g * 8 + s, adam_all, 0.0), axis=1, keepdims=True)
            pre_sum = jnp.sum(jnp.where(lane == s, pre_all, 0.0), axis=1, keepdims=True)
            scale = jnp.sqrt(adam_sum) / (jnp.sqrt(pre_sum) + 1e-06)
            moved = dot(w.pit[...], (w.pre[s] * scale).astype(BF)).astype(BF)
            for r in range(R):
                part = moved[r * NG * NZ:(r + 1) * NG * NZ].reshape(NG, NZ, Q)
                dest[:, k, :, r * Q:(r + 1) * Q] = part

    xpa.recv()
    scaled(range(MAIN), w.par, w.sF)
    xF.start()
    w.rF[pl.ds(me_g, 1)] = w.sF[pl.ds(me_g, 1)]

    norms(range(MAIN, CAP), w.pb)
    xpb.start()
    w.pbr[pl.ds(t, 1)] = w.pb[...]

    xF.recv()
    w.sI[...] = dot(to_zsg, w.rF[...].reshape(places, W)).astype(BF).reshape(NZ, MAIN * NG, W)
    xI.start()
    w.rI[pl.ds(me_z, 1)] = w.sI[pl.ds(me_z, 1)]

    xpb.recv()
    scaled(range(MAIN, CAP), w.pbr, w.sH)
    xH.start()
    w.rH[pl.ds(me_g, 1)] = w.sH[pl.ds(me_g, 1)]

    def factor(s):
        local(lf.at[s], w.lfv.at[s], w.l_lf.at[s]).wait()
        local(rf.at[s], w.rfv.at[s], w.l_rf.at[s]).wait()
        rows = w.gfull[s, pl.ds(shard_rows(t), Q), :]
        gram = lax.dot_general(rows, w.gfull[s], (((1,), (1,)), ((), ())), preferred_element_type=F32)
        w.lnv[s] = (0.9 * w.lfv[s].astype(F32) + 0.1 * gram).astype(BF)
        local(w.lnv.at[s], ln.at[s], w.l_ln.at[s]).start()
        gram = lax.dot_general(w.gown[s], w.gfull[s], (((0,), (0,)), ((), ())), preferred_element_type=F32)
        w.rnv[s] = (0.9 * w.rfv[s].astype(F32) + 0.1 * gram).astype(BF)
        local(w.rnv.at[s], rn.at[s], w.l_rn.at[s]).start()

    for s in range(MAIN):
        factor(s)

    xH.recv()
    flat = [w.rH[:, :, :, r * Q:(r + 1) * Q].reshape(PS, Q) for r in range(R)]
    hits = (held_col == slot_row) & (mz == bz_)
    total = jnp.zeros((PB, Q), F32)
    for r in range(R):
        total += dot(hot(hits & (mr == r)), flat[r])
    w.sJ[...] = total.astype(BF).reshape(NZ, R * CB, Q)
    xJ.start()
    w.rJ[pl.ds(me_z, 1)] = w.sJ[pl.ds(me_z, 1)]

    for s in range(MAIN, CAP):
        factor(s)

    sel_back = hot(key_col == key_main(iota((1, places), 1)))
    xI.recv()
    xJ.recv()
    rest = w.rJ[...].reshape(PB, Q)
    for r in range(R):
        out = dot(sel_back, w.rI[:, :, r * Q:(r + 1) * Q].reshape(places, Q))
        out += dot(hot(rest_col == jnp.where(lrr == r, l_rest, -2)), rest)
        upd[:, r, :, :] = out.astype(BF).reshape(c.NBR, c.NBC, Q)

    for x in (xA, xB, xz, xC, xE, xg, xx, xpa, xpb, xF, xH, xI, xJ):
        x.sent()
    for s in range(CAP):
        for d in (0, 1):
            for copy in (l_first(s, d), l_pass(s, d), g_first(s, d), g_pass(s, d)):
                copy.wait_send()
        local(w.lnv.at[s], ln.at[s], w.l_ln.at[s]).wait()
        local(w.rnv.at[s], rn.at[s], w.l_rn.at[s]).wait()


def per_device(c, grads, second_moment, owner, left_factor, right_factor, left_root, right_root):
    scratch = scratch_of(c)
    vmem, anyw = pl.BlockSpec(memory_space=pltpu.VMEM), pl.BlockSpec(memory_space=pl.ANY)
    like = lambda a: jax.ShapeDtypeStruct(a.shape, a.dtype)
    return pl.pallas_call(
        functools.partial(kernel, c, tuple(scratch)),
        out_shape=(like(grads), like(second_moment), like(left_factor), like(right_factor)),
        in_specs=[vmem, vmem, vmem, anyw, anyw, anyw, anyw],
        out_specs=(vmem, vmem, anyw, anyw),
        scratch_shapes=list(scratch.values()),
        compiler_params=pltpu.CompilerParams(
            collective_id=c.cid, has_side_effects=True, vmem_limit_bytes=48 * 1024 * 1024
        ),
        name="shampoo",
    )(grads, second_moment, owner, left_factor, right_factor, left_root, right_root)


def build(mesh, body):
    rows, cols = P(None, "fsdp", None, "tp"), P("fsdp", "tp", None)
    return jax.shard_map(
        body, mesh=mesh,
        in_specs=(rows, rows, P(), cols, cols, cols, P("fsdp", None, "tp")),
        out_specs=(rows, rows, cols, cols), check_vma=False,
    )


def solution(mesh):
    c = cfg_of(4, 16, 2, 4, 4, 128, 16, 16, 24, 1)
    return build(mesh, functools.partial(per_device, c))
```

```python
import functools
import types

import jax
import jax.numpy as jnp
from jax import lax
from jax.experimental import pallas as pl
from jax.experimental.pallas import tpu as pltpu
from jax.sharding import PartitionSpec as P

BF, F32, I32 = jnp.bfloat16, jnp.float32, jnp.int32
MESH = pl.DeviceIdType.MESH
CAP = 5
MAIN = 2
REST = CAP - MAIN
LANES = 128
VMEM_BYTES = 62 * 1024 * 1024


def cfg_of(NY, NZ, NC, NX, R, Q, NBR, NBC, CB, cid):
    c = types.SimpleNamespace(NY=NY, NZ=NZ, NC=NC, NX=NX, R=R, Q=Q, NBR=NBR, NBC=NBC, CB=CB, cid=cid)
    c.NG = NY * NC
    c.NB = NBR * NBC
    c.B = NX * Q
    c.W = R * Q
    assert c.B == NY * NZ * NC * R
    return c


def idiv(x, d, bound=4096):
    if d & (d - 1) == 0:
        return lax.shift_right_logical(x, jnp.int32(d.bit_length() - 1))
    shift = ((1 << 31) // bound * d).bit_length() - 2
    factor = -(-(1 << shift) // d)
    assert bound * factor < 1 << 31 and (factor * d - (1 << shift)) * bound < 1 << shift
    return lax.shift_right_logical(x * jnp.int32(factor), jnp.int32(shift))


def imod(x, d):
    if d & (d - 1) == 0:
        return x & jnp.int32(d - 1)
    return x - idiv(x, d) * jnp.int32(d)


def iota(shape, dim):
    return lax.broadcasted_iota(I32, shape, dim)


def hot(cond):
    return jnp.where(cond, 1.0, 0.0).astype(BF)


def dot(a, b):
    return jnp.dot(a, b, preferred_element_type=F32)


def scratch_of(c):
    vm = lambda *s: pltpu.VMEM(s, BF)
    vf = lambda *s: pltpu.VMEM(s, F32)
    dma = lambda *s: pltpu.SemaphoreType.DMA(s)
    out = {}
    for name in ("sA", "rA", "sI", "rI"):
        out[name] = vm(c.NZ, MAIN * c.NG, c.W)
    out["zb"] = vm(c.NG, c.NX, c.NZ, c.R * c.CB, c.Q)
    for name in ("sB", "sJ", "rJ"):
        out[name] = vm(c.NZ, c.R * c.CB, c.Q)
    for name in ("sC", "rC", "sF", "rF"):
        out[name] = vm(c.NG, MAIN, c.NZ, c.W)
    for name in ("sH", "rH"):
        out[name] = vm(c.NG, REST, c.NZ, c.W)
    out["pick"] = vm(REST * (c.B // c.NY), c.NC * c.NZ * c.R * c.CB)
    out["gown"] = vm(MAIN, c.B, c.Q)
    out["gfull"] = vm(CAP, c.B, c.B)
    out["lfull"] = vm(CAP, c.B, c.B)
    out["rv"] = vm(CAP, c.B, c.Q)
    for name in ("lfv", "rfv", "lnv", "rnv"):
        out[name] = vm(CAP, c.Q, c.B)
    out["pi"] = vm(c.B, c.B)
    out["pit"] = vm(c.B, c.B)
    out["az"] = vf(c.NZ, 1, LANES)
    out["azr"] = vf(c.NZ, 1, LANES)
    out["wz"] = vf(1, 1, LANES)
    out["wzr"] = vf(c.NZ, 1, LANES)
    for name in ("ag", "wg"):
        out[name] = vf(1, 1, LANES)
        out[name + "r"] = vf(c.NG, 1, LANES)
    for name in ("ax", "pa"):
        out[name] = vf(1, 1, LANES)
        out[name + "r"] = vf(c.NX, 1, LANES)
    for name in ("A", "B", "I", "J", "z", "wz"):
        out["s_" + name], out["r_" + name] = dma(c.NZ), dma(c.NZ)
    for name in ("C", "F", "H", "g", "wg"):
        out["s_" + name], out["r_" + name] = dma(c.NG), dma(c.NG)
    for name in ("x", "pa"):
        out["s_" + name], out["r_" + name] = dma(c.NX), dma(c.NX)
    for name in ("L1", "L2", "G1", "G2"):
        out["s_" + name], out["r_" + name] = dma(CAP, 2), dma(CAP, 2)
    for name in ("X1", "X2", "Y1", "Y2"):
        out["s_" + name], out["r_" + name] = dma(2), dma(2)
    out["s_K"], out["r_K"] = dma(c.NY), dma(c.NY)
    for name in ("l_lf", "l_rf", "l_rv", "l_lr", "l_ln", "l_rn"):
        out[name] = dma(CAP)
    out["upd"] = vm(c.NBR, c.R, c.NBC, c.Q)
    out["mom"] = vm(c.NBR, c.R, c.NBC, c.Q)
    out["l_out"] = dma(2)
    out["grads"] = vm(c.NBR, c.R, c.NBC, c.Q)
    out["sm"] = vm(c.NBR, c.R, c.NBC, c.Q)
    out["owner"] = pltpu.VMEM((c.NBR, c.NBC), I32)
    out["l_in"] = dma(3)
    return out


def kernel(c, names, grads_in, sm_in, owner_in, lf, rf, lr, rr, upd_out, mom_out, ln, rn, left_out, *scratch):
    w = types.SimpleNamespace(**dict(zip(names, scratch)))
    NZ, NG, NX, NB, R, Q, B, W, CB = c.NZ, c.NG, c.NX, c.NB, c.R, c.Q, c.B, c.W, c.CB
    grads, sm, owner, upd, mom = w.grads, w.sm, w.owner, w.upd, w.mom
    outputs = [pltpu.make_async_copy(mom, mom_out, w.l_out.at[0]), pltpu.make_async_copy(upd, upd_out, w.l_out.at[1])]
    inputs = [
        pltpu.make_async_copy(a, b, w.l_in.at[k])
        for k, (a, b) in enumerate(((owner_in, owner), (grads_in, grads), (sm_in, sm)))
    ]
    for copy in inputs:
        copy.start()
    f = lax.axis_index("fsdp")
    t = lax.axis_index("tp")
    me_c = lax.rem(f, c.NC)
    me_z = lax.rem(lax.div(f, c.NC), NZ)
    me_y = lax.div(f, c.NC * NZ)
    me_g = me_y * c.NC + me_c
    right, left = lax.rem(t + 1, NX), lax.rem(t + NX - 1, NX)

    def at_z(z):
        return {"fsdp": (me_y * NZ + z) * c.NC + me_c, "tp": t}

    def at_g(g):
        return {"fsdp": (lax.div(g, c.NC) * NZ + me_z) * c.NC + lax.rem(g, c.NC), "tp": t}

    def at_x(x):
        return {"fsdp": f, "tp": x}

    def rcopy(src, dst, ssem, rsem, dev):
        return pltpu.make_async_remote_copy(
            src_ref=src, dst_ref=dst, send_sem=ssem, recv_sem=rsem, device_id=dev, device_id_type=MESH
        )

    def loop(lo, hi, body):
        def step(k, carry):
            body(k)
            return carry
        lax.fori_loop(lo, hi, step, 0)

    def each_z(body):
        half = NZ // 2
        body(lax.rem(me_z + half, NZ))
        if half > 1:
            def pair(k):
                d = half - 1 - k
                body(lax.rem(me_z + d, NZ))
                body(lax.rem(me_z + NZ - d, NZ))
            loop(0, half - 1, pair)

    def each_g(body):
        loop(1, NG, lambda k: body(lax.rem(me_g + k, NG)))

    def each_x(body):
        loop(1, NX, lambda k: body(lax.rem(t + k, NX)))

    class Exchange:
        def __init__(self, each, at, me, src, dst, sems):
            self.each, self.at, self.me, self.src, self.dst = each, at, me, src, dst
            self.ss, self.rs = getattr(w, "s_" + sems), getattr(w, "r_" + sems)

        def start(self):
            def go(p):
                rcopy(self.src(p), self.dst.at[self.me], self.ss.at[p], self.rs.at[self.me], self.at(p)).start()
            self.each(go)

        def recv(self):
            def go(p):
                rcopy(self.src(p), self.dst.at[p], self.ss.at[p], self.rs.at[p], self.at(p)).wait_recv()
            self.each(go)

        def sent(self):
            def go(p):
                rcopy(self.src(p), self.dst.at[p], self.ss.at[p], self.rs.at[p], self.at(p)).wait_send()
            self.each(go)

    def one(buf):
        return lambda p: buf.at[0]

    def many(buf):
        return lambda p: buf.at[p]

    xA = Exchange(each_z, at_z, me_z, many(w.sA), w.rA, "A")
    xB = Exchange(each_z, at_z, me_z, many(w.sB), w.zb.at[me_g, t], "B")
    xI = Exchange(each_z, at_z, me_z, many(w.sI), w.rI, "I")
    xJ = Exchange(each_z, at_z, me_z, many(w.sJ), w.rJ, "J")
    xz = Exchange(each_z, at_z, me_z, many(w.az), w.azr, "z")
    xC = Exchange(each_g, at_g, me_g, many(w.sC), w.rC, "C")
    xF = Exchange(each_g, at_g, me_g, many(w.sF), w.rF, "F")
    xH = Exchange(each_g, at_g, me_g, many(w.sH), w.rH, "H")
    xg = Exchange(each_g, at_g, me_g, one(w.ag), w.agr, "g")
    xx = Exchange(each_x, at_x, t, one(w.ax), w.axr, "x")
    xpa = Exchange(each_x, at_x, t, one(w.pa), w.par, "pa")
    xwg = Exchange(each_g, at_g, me_g, one(w.wg), w.wgr, "wg")
    xwz = Exchange(each_z, at_z, me_z, one(w.wz), w.wzr, "wz")

    def shard_rows(x):
        return pl.multiple_of(x * Q, Q)

    def l_first(s, d):
        dst = w.lfull.at[s, pl.ds(shard_rows(t), Q), :]
        return rcopy(lr.at[s], dst, w.s_L1.at[s, d], w.r_L1.at[s, d], at_x(right if d == 0 else left))

    def l_pass(s, d):
        x = left if d == 0 else right
        part = w.lfull.at[s, pl.ds(pl.multiple_of(x * Q + d * (Q // 2), Q // 2), Q // 2), :]
        return rcopy(part, part, w.s_L2.at[s, d], w.r_L2.at[s, d], at_x(right if d == 0 else left))

    def g_first(s, d):
        dst = w.gfull.at[s, :, pl.ds(shard_rows(t), Q)]
        return rcopy(w.gown.at[s], dst, w.s_G1.at[s, d], w.r_G1.at[s, d], at_x(right if d == 0 else left))

    def g_pass(s, d):
        x = left if d == 0 else right
        part = w.gfull.at[s, pl.ds(d * (B // 2), B // 2), pl.ds(shard_rows(x), Q)]
        return rcopy(part, part, w.s_G2.at[s, d], w.r_G2.at[s, d], at_x(right if d == 0 else left))

    def pass_on(first, onward, *s):
        for d in (0, 1):
            first(*s, d).wait_recv()
            onward(*s, d).start()

    up, down = lax.rem(me_y + 1, c.NY), lax.rem(me_y + c.NY - 1, c.NY)

    def b_copy(part, name, k, dev):
        sems = getattr(w, "s_" + name), getattr(w, "r_" + name)
        return rcopy(part, part, sems[0].at[k], sems[1].at[k], dev)

    def bx_first(d):
        return b_copy(w.zb.at[me_g, t], "X1", d, at_x(right if d == 0 else left))

    def bx_pass(d):
        part = w.zb.at[me_g, left if d == 0 else right, pl.ds(d * (NZ // 2), NZ // 2)]
        return b_copy(part, "X2", d, at_x(right if d == 0 else left))

    def at_y(y):
        return at_g(y * c.NC + me_c)

    def by_first(d):
        return b_copy(w.zb.at[me_g], "Y1", d, at_y(up if d == 0 else down))

    def by_pass(d):
        part = w.zb.at[(down if d == 0 else up) * c.NC + me_c, pl.ds(d * (NX // 2), NX // 2)]
        return b_copy(part, "Y2", d, at_y(up if d == 0 else down))

    def b_core(k):
        y = lax.rem(me_y + k, c.NY)
        return b_copy(w.zb.at[y * c.NC + me_c], "K", k, at_g(me_y * c.NC + (1 - me_c)))

    def b_core_in(k):
        y = lax.rem(me_y + k, c.NY)
        return b_copy(w.zb.at[y * c.NC + (1 - me_c)], "K", k, at_g(me_y * c.NC + (1 - me_c)))

    barrier = pltpu.get_barrier_semaphore()

    def greet(at):
        def go(p):
            pl.semaphore_signal(barrier, inc=1, device_id=at(p), device_id_type=MESH)
        return go
    each_z(greet(at_z))
    each_g(greet(at_g))
    each_x(greet(at_x))

    def local(src, dst, sem):
        return pltpu.make_async_copy(src, dst, sem)

    def l_own(s):
        return local(lr.at[s], w.lfull.at[s, pl.ds(shard_rows(t), Q), :], w.l_lr.at[s])

    def loads(s):
        return (
            local(rr.at[s], w.rv.at[s], w.l_rv.at[s]),
            local(lf.at[s], w.lfv.at[s], w.l_lf.at[s]),
            local(rf.at[s], w.rfv.at[s], w.l_rf.at[s]),
        )

    inputs[0].wait()
    spread = hot(imod(iota((c.NBC, NB), 1), c.NBC) == iota((c.NBC, NB), 0))
    wide = dot(owner[...].astype(F32).astype(BF), spread)
    own_row = jnp.sum(
        jnp.where(idiv(iota((c.NBR, NB), 1), c.NBC) == iota((c.NBR, NB), 0), wide, 0.0), axis=0, keepdims=True
    )
    i0, i1 = iota((NB, NB), 0), iota((NB, NB), 1)
    own_col = jnp.sum(jnp.where(i0 == i1, own_row, 0.0), axis=1, keepdims=True)
    same = own_row == own_col
    rank_row = jnp.sum(jnp.where(same & (i0 < i1), 1.0, 0.0), axis=0, keepdims=True).astype(I32)
    rank_col = jnp.sum(jnp.where(same & (i1 < i0), 1.0, 0.0), axis=1, keepdims=True).astype(I32)
    own_row, own_col = own_row.astype(I32), own_col.astype(I32)
    key_row, key_col = own_row * 8 + rank_row, own_col * 8 + rank_col
    z_row, z_col = imod(idiv(own_row, c.NC), NZ), imod(idiv(own_col, c.NC), NZ)

    def key_of(z, g, s):
        return ((idiv(g, c.NC) * NZ + z) * c.NC + imod(g, c.NC)) * 8 + s

    def key_main(m):
        return key_of(idiv(m, MAIN * NG), imod(m, NG), imod(idiv(m, NG), MAIN))

    places = NZ * MAIN * NG
    sel_main = hot(key_main(iota((places, 1), 0)) == key_row)
    inputs[1].wait()
    for r in range(R):
        block = grads[:, r, :, :].reshape(NB, Q)
        w.sA[:, :, r * Q:(r + 1) * Q] = dot(sel_main, block).astype(BF).reshape(NZ, MAIN * NG, Q)

    pl.semaphore_wait(barrier, NZ - 1 + NG - 1 + NX - 1)
    xA.start()
    for s in range(MAIN):
        for d in (0, 1):
            l_first(s, d).start()

    over_row, over_col = rank_row >= MAIN, rank_col >= MAIN
    mates = (z_row == z_col)
    pos_row = jnp.sum(jnp.where(mates & over_col & (i0 < i1), 1.0, 0.0), axis=0, keepdims=True).astype(I32)
    pos_col = jnp.sum(jnp.where(mates & over_row & (i1 < i0), 1.0, 0.0), axis=1, keepdims=True).astype(I32)
    PB = NZ * R * CB
    left_out[0] = jnp.sum(jnp.where(over_row & (pos_row >= CB), 1, 0))
    rest_row = jnp.where(over_row & (pos_row < CB), z_row * CB + pos_row, -1)
    rest_col = jnp.where(over_col & (pos_col < CB), z_col * CB + pos_col, -1)

    def rest_parts(m):
        return idiv(m, R * CB), imod(idiv(m, CB), R), imod(m, CB)

    mz, mr, mb = rest_parts(iota((PB, 1), 0))
    lz, lrr, lb = rest_parts(iota((1, PB), 1))
    m_rest, l_rest = mz * CB + mb, lz * CB + lb
    total = jnp.zeros((PB, Q), F32)
    for r in range(R):
        sel = hot(jnp.where(mr == r, m_rest, -2) == rest_row)
        total += dot(sel, grads[:, r, :, :].reshape(NB, Q))
    w.sB[...] = total.astype(BF).reshape(NZ, R * CB, Q)
    xB.start()
    w.rA[pl.ds(me_z, 1)] = w.sA[pl.ds(me_z, 1)]
    w.zb[pl.ds(me_g, 1), pl.ds(t, 1), pl.ds(me_z, 1)] = w.sB[pl.ds(me_z, 1)][None, None]
    for s in range(CAP):
        l_own(s).start()
        for copy in loads(s):
            copy.start()

    inputs[2].wait()
    adam_col = jnp.zeros((NB, 1), F32)
    for r in range(R):
        g = grads[:, r, :, :].astype(F32)
        moment = 0.95 * sm[:, r, :, :].astype(F32) + 0.05 * g * g
        mom[:, r, :, :] = moment.astype(BF)
        adam = g / (jnp.sqrt(moment) + 1e-08)
        adam_col += jnp.sum((adam * adam).reshape(NB, Q), axis=1, keepdims=True)
    outputs[0].start()
    lane = iota((1, LANES), 1)
    lane_key = jnp.where(lane < NG * 8, key_of(jnp.zeros_like(lane), idiv(lane, 8), imod(lane, 8)), -1)

    def sums_for(z):
        hit = (key_col - z * (c.NC * 8)) == lane_key
        w.az[pl.ds(z, 1)] = jnp.sum(jnp.where(hit, adam_col, 0.0), axis=0, keepdims=True)[None]
    loop(0, NZ, sums_for)
    xz.start()
    w.azr[pl.ds(me_z, 1)] = w.az[pl.ds(me_z, 1)]

    def natural(m):
        r, g, z = idiv(m, NG * NZ), imod(idiv(m, NZ), NG), imod(m, NZ)
        return ((idiv(g, c.NC) * NZ + z) * c.NC + imod(g, c.NC)) * R + r
    w.pi[...] = hot(iota((B, B), 0) == natural(iota((1, B), 1)))
    w.pit[...] = hot(natural(iota((B, 1), 0)) == iota((B, B), 1))

    def turned(m):
        return (imod(m, NZ) * MAIN + imod(idiv(m, NZ), MAIN)) * NG + idiv(m, NZ * MAIN)
    to_gsz = hot(turned(iota((places, 1), 0)) == iota((places, places), 1))
    to_zsg = hot(iota((places, places), 0) == turned(iota((1, places), 1)))

    gm = iota((1, c.NC * PB), 1)
    gc = idiv(gm, PB)
    gz, gr, gb = rest_parts(gm - gc * PB)
    held_row = jnp.sum(
        jnp.where(rest_col == me_z * CB + gb, key_col + 1, 0), axis=0, keepdims=True
    ) - 1
    held_col = jnp.sum(
        jnp.where(me_z * CB + mb == rest_row, key_row + 1, 0), axis=1, keepdims=True
    ) - 1

    def rest_slots(m):
        return idiv(m, REST * NZ), imod(idiv(m, NZ), REST) + MAIN, imod(m, NZ)
    PS = NG * REST * NZ
    bg_, bs_, bz_ = rest_slots(iota((1, PS), 1))
    slot_row = key_of(me_z, bg_, bs_)

    per_y = c.B // c.NY
    n = iota((REST * per_y, 1), 0)
    slot = idiv(n, per_y)
    n = n - slot * per_y
    n_z, n_c, n_r = idiv(n, c.NC * R), imod(idiv(n, R), c.NC), imod(n, R)
    wanted = key_of(me_z, me_g, slot + MAIN)
    w.pick[...] = hot((held_row == wanted) & (gz == n_z) & (gc == n_c) & (gr == n_r))
    for s in range(MAIN):
        pass_on(l_first, l_pass, s)

    for s in range(MAIN, CAP):
        for d in (0, 1):
            l_first(s, d).start()
    xA.recv()
    w.sC[...] = dot(to_gsz, w.rA[...].reshape(places, W)).astype(BF).reshape(NG, MAIN, NZ, W)
    xC.start()
    w.rC[pl.ds(me_g, 1)] = w.sC[pl.ds(me_g, 1)]

    xB.recv()
    for d in (0, 1):
        bx_first(d).start()

    xC.recv()
    for s in range(MAIN):
        rows = [w.rC[:, s, :, r * Q:(r + 1) * Q].reshape(NG * NZ, Q) for r in range(R)]
        cols = dot(w.pi[...], jnp.concatenate(rows, axis=0)).astype(BF)
        w.gown[s] = cols
        w.gfull[s, :, pl.ds(shard_rows(t), Q)] = cols
    pass_on(bx_first, bx_pass)
    for s in range(MAIN):
        for d in (0, 1):
            g_first(s, d).start()

    for d in (0, 1):
        bx_pass(d).wait_recv()
    for d in (0, 1):
        by_first(d).start()
    b_core(0).start()

    for s in range(MAIN):
        pass_on(g_first, g_pass, s)

    for s in range(MAIN, CAP):
        pass_on(l_first, l_pass, s)

    pass_on(by_first, by_pass)
    b_core(1).start()
    b_core(c.NY - 1).start()

    norm_row = jnp.zeros((1, LANES), F32)

    def precond(s, dest, at):
        l_own(s).wait()
        local(rr.at[s], w.rv.at[s], w.l_rv.at[s]).wait()
        for d in (0, 1):
            l_pass(s, d).wait_recv()
            if s < MAIN:
                g_pass(s, d).wait_recv()
        cols = dot(w.gfull[s], w.rv[s])
        high = cols.astype(BF)
        low = (cols - high.astype(F32)).astype(BF)
        out = (dot(w.lfull[s], high) + dot(w.lfull[s], low)).astype(BF)
        moved = dot(w.pit[...], out).astype(BF)
        for r in range(R):
            dest[:, at, :, r * Q:(r + 1) * Q] = moved[r * NG * NZ:(r + 1) * NG * NZ].reshape(NG, NZ, Q)
        wide_out = out.astype(F32)
        total = jnp.sum(jnp.sum(wide_out * wide_out, axis=0, keepdims=True), axis=1, keepdims=True)
        return jnp.where(lane == s, total, norm_row)

    for s in range(MAIN):
        norm_row = precond(s, w.sF, s)
    xF.start()
    w.rF[pl.ds(me_g, 1)] = w.sF[pl.ds(me_g, 1)]

    for d in (0, 1):
        by_pass(d).wait_recv()
    b_core(2).start()

    xz.recv()
    w.ag[...] = jnp.sum(w.azr[...], axis=0, keepdims=True)
    xg.start()
    w.agr[pl.ds(me_g, 1)] = w.ag[...]

    for k in range(c.NY):
        b_core_in(k).wait_recv()

    def place(y):
        parts = [
            jnp.concatenate([w.zb[y * c.NC + k, x].reshape(PB, Q) for x in range(NX)], axis=1)
            for k in range(c.NC)
        ]
        got = dot(w.pick[...], jnp.concatenate(parts, axis=0)).astype(BF)
        for k in range(REST):
            rows = pl.ds(pl.multiple_of(y * per_y, per_y), per_y)
            w.gfull[MAIN + k, rows, :] = got[k * per_y:(k + 1) * per_y]
    loop(0, c.NY, place)

    xF.recv()
    w.sI[...] = dot(to_zsg, w.rF[...].reshape(places, W)).astype(BF).reshape(NZ, MAIN * NG, W)
    xI.start()
    w.rI[pl.ds(me_z, 1)] = w.sI[pl.ds(me_z, 1)]

    for s in range(MAIN, CAP):
        norm_row = precond(s, w.sH, s - MAIN)
    xH.start()
    w.rH[pl.ds(me_g, 1)] = w.sH[pl.ds(me_g, 1)]
    w.pa[...] = norm_row[None]
    xpa.start()
    w.par[pl.ds(t, 1)] = w.pa[...]

    xg.recv()
    w.ax[...] = jnp.sum(w.agr[...], axis=0, keepdims=True)
    xx.start()
    w.axr[pl.ds(t, 1)] = w.ax[...]
    def factor(s):
        local(lf.at[s], w.lfv.at[s], w.l_lf.at[s]).wait()
        local(rf.at[s], w.rfv.at[s], w.l_rf.at[s]).wait()
        rows = w.gfull[s, pl.ds(shard_rows(t), Q), :]
        gram = lax.dot_general(rows, w.gfull[s], (((1,), (1,)), ((), ())), preferred_element_type=F32)
        w.lnv[s] = (0.9 * w.lfv[s].astype(F32) + 0.1 * gram).astype(BF)
        local(w.lnv.at[s], ln.at[s], w.l_ln.at[s]).start()
        cols = w.gfull[s, :, pl.ds(shard_rows(t), Q)]
        gram = lax.dot_general(cols, w.gfull[s], (((0,), (0,)), ((), ())), preferred_element_type=F32)
        w.rnv[s] = (0.9 * w.rfv[s].astype(F32) + 0.1 * gram).astype(BF)
        local(w.rnv.at[s], rn.at[s], w.l_rn.at[s]).start()

    for s in range(MAIN):
        factor(s)

    xx.recv()
    xpa.recv()
    adam_all = jnp.sum(w.axr[...], axis=0)
    norm_all = jnp.sum(w.par[...], axis=0)
    scales = jnp.zeros((1, LANES), F32)
    for s in range(CAP):
        adam_sum = jnp.sum(jnp.where(lane == me_g * 8 + s, adam_all, 0.0), axis=1, keepdims=True)
        norm_sum = jnp.sum(jnp.where(lane == s, norm_all, 0.0), axis=1, keepdims=True)
        scale = jnp.sqrt(adam_sum) / (jnp.sqrt(norm_sum) + 1e-06)
        scales = jnp.where(lane == me_g * 8 + s, scale, scales)
    w.wg[...] = scales[None]
    xwg.start()
    w.wgr[pl.ds(me_g, 1)] = w.wg[...]

    xH.recv()
    flat = [w.rH[:, :, :, r * Q:(r + 1) * Q].reshape(PS, Q) for r in range(R)]
    hits = (held_col == slot_row) & (mz == bz_)
    total = jnp.zeros((PB, Q), F32)
    for r in range(R):
        total += dot(hot(hits & (mr == r)), flat[r])
    w.sJ[...] = total.astype(BF).reshape(NZ, R * CB, Q)
    xJ.start()
    w.rJ[pl.ds(me_z, 1)] = w.sJ[pl.ds(me_z, 1)]

    xwg.recv()
    w.wz[...] = jnp.sum(w.wgr[...], axis=0, keepdims=True)
    xwz.start()
    w.wzr[pl.ds(me_z, 1)] = w.wz[...]

    for s in range(MAIN, CAP):
        factor(s)

    sel_back = hot(key_col == key_main(iota((1, places), 1)))
    xI.recv()
    main_part = [dot(sel_back, w.rI[:, :, r * Q:(r + 1) * Q].reshape(places, Q)) for r in range(R)]
    xwz.recv()

    def scale_of(z, total):
        return total + jnp.where((key_col - z * (c.NC * 8)) == lane_key, w.wzr[z], 0.0)
    scale_col = jnp.sum(
        lax.fori_loop(0, NZ, scale_of, jnp.zeros((NB, LANES), F32)), axis=1, keepdims=True
    )
    xJ.recv()
    rest = w.rJ[...].reshape(PB, Q)
    for r in range(R):
        out = main_part[r] + dot(hot(rest_col == jnp.where(lrr == r, l_rest, -2)), rest)
        upd[:, r, :, :] = (out * scale_col).astype(BF).reshape(c.NBR, c.NBC, Q)

    outputs[1].start()
    for copy in outputs:
        copy.wait()
    for x in (xA, xB, xz, xC, xg, xx, xpa, xF, xH, xI, xJ, xwg, xwz):
        x.sent()
    for d in (0, 1):
        for copy in (bx_first(d), bx_pass(d), by_first(d), by_pass(d)):
            copy.wait_send()
        for s in range(CAP):
            l_first(s, d).wait_send()
            l_pass(s, d).wait_send()
        for s in range(MAIN):
            g_first(s, d).wait_send()
            g_pass(s, d).wait_send()
    for k in range(c.NY):
        b_core(k).wait_send()
    for s in range(CAP):
        local(w.lnv.at[s], ln.at[s], w.l_ln.at[s]).wait()
        local(w.rnv.at[s], rn.at[s], w.l_rn.at[s]).wait()


def finish(results):
    count = len(results)

    def body(*refs):
        ins, outs, held, (got, put) = refs[:count], refs[count:2 * count], refs[2 * count:3 * count], refs[3 * count:]
        arrays = list(enumerate(zip(ins, held, outs)))
        for k, (a, v, _) in arrays:
            pltpu.make_async_copy(a, v, got.at[k]).start()
        for k, (a, v, o) in arrays:
            pltpu.make_async_copy(a, v, got.at[k]).wait()
            pltpu.make_async_copy(v, o, put.at[k]).start()
        for k, (_, v, o) in arrays:
            pltpu.make_async_copy(v, o, put.at[k]).wait()
    hbm = pl.BlockSpec(memory_space=pltpu.HBM)
    return tuple(pl.pallas_call(
        body,
        out_shape=tuple(jax.ShapeDtypeStruct(a.shape, a.dtype) for a in results),
        in_specs=[hbm] * count,
        out_specs=(hbm,) * count,
        scratch_shapes=[pltpu.VMEM(a.shape, a.dtype) for a in results] + [pltpu.SemaphoreType.DMA((count,))] * 2,
        compiler_params=pltpu.CompilerParams(vmem_limit_bytes=VMEM_BYTES),
        name="finish",
    )(*results))


def step(c, grads, second_moment, owner, left_factor, right_factor, left_root, right_root):
    scratch = scratch_of(c)
    vmem, hbm = pl.BlockSpec(memory_space=pltpu.VMEM), pl.BlockSpec(memory_space=pltpu.HBM)
    smem = pl.BlockSpec(memory_space=pltpu.SMEM)
    like = lambda a: jax.ShapeDtypeStruct(a.shape, a.dtype)
    return pl.pallas_call(
        functools.partial(kernel, c, tuple(scratch)),
        out_shape=(
            like(grads), like(second_moment), like(left_factor), like(right_factor),
            jax.ShapeDtypeStruct((1,), I32),
        ),
        in_specs=[hbm] * 7,
        out_specs=(hbm, hbm, hbm, hbm, smem),
        scratch_shapes=list(scratch.values()),
        compiler_params=pltpu.CompilerParams(
            collective_id=c.cid, has_side_effects=True, vmem_limit_bytes=VMEM_BYTES
        ),
        name="shampoo",
    )(grads, second_moment, owner, left_factor, right_factor, left_root, right_root)


def per_device(few, enough, *args):
    *results, left_out = step(few, *args)
    return lax.cond(
        left_out[0] == 0,
        lambda: finish(results),
        lambda: finish(step(enough, *args)[:4]),
    )


def build(mesh, body):
    rows, cols = P(None, "fsdp", None, "tp"), P("fsdp", "tp", None)
    return jax.shard_map(
        body, mesh=mesh,
        in_specs=(rows, rows, P(), cols, cols, cols, P("fsdp", None, "tp")),
        out_specs=(rows, rows, cols, cols), check_vma=False,
    )


def solution(mesh):
    few = cfg_of(4, 16, 2, 4, 4, 128, 16, 16, 4, 1)
    enough = cfg_of(4, 16, 2, 4, 4, 128, 16, 16, 24, 2)
    return build(mesh, functools.partial(per_device, few, enough))
```

```python
import functools
import types

import jax
import jax.numpy as jnp
from jax import lax
from jax.experimental import pallas as pl
from jax.experimental.pallas import tpu as pltpu
from jax.sharding import PartitionSpec as P

BF, F32, I32 = jnp.bfloat16, jnp.float32, jnp.int32
MESH = pl.DeviceIdType.MESH
CAP = 5
MAIN = 2
REST = CAP - MAIN
LANES = 128
VMEM_BYTES = 62 * 1024 * 1024


def cfg_of(NY, NZ, NC, NX, R, Q, NBR, NBC, CB, cid):
    c = types.SimpleNamespace(NY=NY, NZ=NZ, NC=NC, NX=NX, R=R, Q=Q, NBR=NBR, NBC=NBC, CB=CB, cid=cid)
    c.NG = NY * NC
    c.NB = NBR * NBC
    c.B = NX * Q
    c.W = R * Q
    assert c.B == NY * NZ * NC * R
    return c


def idiv(x, d, bound=4096):
    if d & (d - 1) == 0:
        return lax.shift_right_logical(x, jnp.int32(d.bit_length() - 1))
    shift = ((1 << 31) // bound * d).bit_length() - 2
    factor = -(-(1 << shift) // d)
    assert bound * factor < 1 << 31 and (factor * d - (1 << shift)) * bound < 1 << shift
    return lax.shift_right_logical(x * jnp.int32(factor), jnp.int32(shift))


def imod(x, d):
    if d & (d - 1) == 0:
        return x & jnp.int32(d - 1)
    return x - idiv(x, d) * jnp.int32(d)


def iota(shape, dim):
    return lax.broadcasted_iota(I32, shape, dim)


def hot(cond):
    return jnp.where(cond, 1.0, 0.0).astype(BF)


def dot(a, b):
    return jnp.dot(a, b, preferred_element_type=F32)


def scratch_of(c):
    vm = lambda *s: pltpu.VMEM(s, BF)
    vf = lambda *s: pltpu.VMEM(s, F32)
    dma = lambda *s: pltpu.SemaphoreType.DMA(s)
    out = {}
    for name in ("sA", "rA", "sI", "rI"):
        out[name] = vm(c.NZ, MAIN * c.NG, c.W)
    out["zb"] = vm(c.NG, c.NX, c.NZ, c.R * c.CB, c.Q)
    for name in ("sB", "sJ", "rJ"):
        out[name] = vm(c.NZ, c.R * c.CB, c.Q)
    for name in ("sC", "rC", "sF", "rF"):
        out[name] = vm(c.NG, MAIN, c.NZ, c.W)
    for name in ("sH", "rH"):
        out[name] = vm(c.NG, REST, c.NZ, c.W)
    out["pick"] = vm(REST * (c.B // c.NY), c.NC * c.NZ * c.R * c.CB)
    out["gown"] = vm(MAIN, c.B, c.Q)
    out["gfull"] = vm(CAP, c.B, c.B)
    out["lfull"] = vm(CAP, c.B, c.B)
    out["rv"] = vm(CAP, c.B, c.Q)
    for name in ("lfv", "rfv", "lnv", "rnv"):
        out[name] = vm(CAP, c.Q, c.B)
    out["pi"] = vm(c.B, c.B)
    out["pit"] = vm(c.B, c.B)
    out["az"] = vf(c.NZ, 1, LANES)
    out["azr"] = vf(c.NZ, 1, LANES)
    out["wz"] = vf(1, 1, LANES)
    out["wzr"] = vf(c.NZ, 1, LANES)
    for name in ("ag", "wg"):
        out[name] = vf(1, 1, LANES)
        out[name + "r"] = vf(c.NG, 1, LANES)
    for name in ("ax", "pa"):
        out[name] = vf(1, 1, LANES)
        out[name + "r"] = vf(c.NX, 1, LANES)
    for name in ("A", "B", "I", "J", "z", "wz"):
        out["s_" + name], out["r_" + name] = dma(1), dma(1)
    for name in ("C", "F", "H", "g", "wg"):
        out["s_" + name], out["r_" + name] = dma(1), dma(1)
    for name in ("x", "pa"):
        out["s_" + name], out["r_" + name] = dma(1), dma(1)
    for name in ("L1", "L2", "G1", "G2"):
        out["s_" + name], out["r_" + name] = dma(CAP, 2), dma(CAP, 2)
    for name in ("X1", "X2", "Y1", "Y2"):
        out["s_" + name], out["r_" + name] = dma(2), dma(2)
    out["s_K"], out["r_K"] = dma(c.NY), dma(c.NY)
    for name in ("l_lf", "l_rf", "l_rv", "l_lr", "l_ln", "l_rn"):
        out[name] = dma(1)
    out["upd"] = vm(c.NBR, c.R, c.NBC, c.Q)
    out["mom"] = vm(c.NBR, c.R, c.NBC, c.Q)
    out["l_out"] = dma(2)
    out["grads"] = vm(c.NBR, c.R, c.NBC, c.Q)
    out["sm"] = vm(c.NBR, c.R, c.NBC, c.Q)
    out["owner"] = pltpu.VMEM((c.NBR, c.NBC), I32)
    out["l_in"] = dma(3)
    return out


def kernel(c, names, grads_in, sm_in, owner_in, lf, rf, lr, rr, upd_out, mom_out, ln, rn, left_out, *scratch):
    w = types.SimpleNamespace(**dict(zip(names, scratch)))
    NZ, NG, NX, NB, R, Q, B, W, CB = c.NZ, c.NG, c.NX, c.NB, c.R, c.Q, c.B, c.W, c.CB
    grads, sm, owner, upd, mom = w.grads, w.sm, w.owner, w.upd, w.mom
    outputs = [pltpu.make_async_copy(mom, mom_out, w.l_out.at[0]), pltpu.make_async_copy(upd, upd_out, w.l_out.at[1])]
    inputs = [
        pltpu.make_async_copy(a, b, w.l_in.at[k])
        for k, (a, b) in enumerate(((owner_in, owner), (grads_in, grads), (sm_in, sm)))
    ]
    for copy in inputs:
        copy.start()
    f = lax.axis_index("fsdp")
    t = lax.axis_index("tp")
    me_c = lax.rem(f, c.NC)
    me_z = lax.rem(lax.div(f, c.NC), NZ)
    me_y = lax.div(f, c.NC * NZ)
    me_g = me_y * c.NC + me_c
    right, left = lax.rem(t + 1, NX), lax.rem(t + NX - 1, NX)

    def at_z(z):
        return {"fsdp": (me_y * NZ + z) * c.NC + me_c, "tp": t}

    def at_g(g):
        return {"fsdp": (lax.div(g, c.NC) * NZ + me_z) * c.NC + lax.rem(g, c.NC), "tp": t}

    def at_x(x):
        return {"fsdp": f, "tp": x}

    def rcopy(src, dst, ssem, rsem, dev):
        return pltpu.make_async_remote_copy(
            src_ref=src, dst_ref=dst, send_sem=ssem, recv_sem=rsem, device_id=dev, device_id_type=MESH
        )

    def loop(lo, hi, body):
        def step(k, carry):
            body(k)
            return carry
        lax.fori_loop(lo, hi, step, 0)

    def each_z(body):
        half = NZ // 2
        body(lax.rem(me_z + half, NZ))
        if half > 1:
            def pair(k):
                d = half - 1 - k
                body(lax.rem(me_z + d, NZ))
                body(lax.rem(me_z + NZ - d, NZ))
            loop(0, half - 1, pair)

    def each_g(body):
        loop(1, NG, lambda k: body(lax.rem(me_g + k, NG)))

    def each_x(body):
        loop(1, NX, lambda k: body(lax.rem(t + k, NX)))

    class Exchange:
        def __init__(self, each, at, me, src, dst, sems):
            self.each, self.at, self.me, self.src, self.dst = each, at, me, src, dst
            self.ss, self.rs = getattr(w, "s_" + sems).at[0], getattr(w, "r_" + sems).at[0]
            self.count = {each_z: NZ, each_g: NG, each_x: NX}[each]

        def start(self):
            def go(p):
                rcopy(self.src(p), self.dst.at[self.me], self.ss, self.rs, self.at(p)).start()
            self.each(go)

        def all(self):
            whole = self.dst.at[pl.ds(0, self.count - 1)]
            return rcopy(whole, whole, self.ss, self.rs, self.at(lax.rem(self.me + 1, self.count)))

        def recv(self):
            self.all().wait_recv()

        def sent(self):
            self.all().wait_send()

    def one(buf):
        return lambda p: buf.at[0]

    def many(buf):
        return lambda p: buf.at[p]

    xA = Exchange(each_z, at_z, me_z, many(w.sA), w.rA, "A")
    xB = Exchange(each_z, at_z, me_z, many(w.sB), w.zb.at[me_g, t], "B")
    xI = Exchange(each_z, at_z, me_z, many(w.sI), w.rI, "I")
    xJ = Exchange(each_z, at_z, me_z, many(w.sJ), w.rJ, "J")
    xz = Exchange(each_z, at_z, me_z, many(w.az), w.azr, "z")
    xC = Exchange(each_g, at_g, me_g, many(w.sC), w.rC, "C")
    xF = Exchange(each_g, at_g, me_g, many(w.sF), w.rF, "F")
    xH = Exchange(each_g, at_g, me_g, many(w.sH), w.rH, "H")
    xg = Exchange(each_g, at_g, me_g, one(w.ag), w.agr, "g")
    xx = Exchange(each_x, at_x, t, one(w.ax), w.axr, "x")
    xpa = Exchange(each_x, at_x, t, one(w.pa), w.par, "pa")
    xwg = Exchange(each_g, at_g, me_g, one(w.wg), w.wgr, "wg")
    xwz = Exchange(each_z, at_z, me_z, one(w.wz), w.wzr, "wz")

    def shard_rows(x):
        return pl.multiple_of(x * Q, Q)

    def l_first(s, d):
        dst = w.lfull.at[s, pl.ds(shard_rows(t), Q), :]
        return rcopy(lr.at[s], dst, w.s_L1.at[s, d], w.r_L1.at[s, d], at_x(right if d == 0 else left))

    def l_pass(s, d):
        x = left if d == 0 else right
        part = w.lfull.at[s, pl.ds(pl.multiple_of(x * Q + d * (Q // 2), Q // 2), Q // 2), :]
        return rcopy(part, part, w.s_L2.at[s, d], w.r_L2.at[s, d], at_x(right if d == 0 else left))

    def g_first(s, d):
        dst = w.gfull.at[s, :, pl.ds(shard_rows(t), Q)]
        return rcopy(w.gown.at[s], dst, w.s_G1.at[s, d], w.r_G1.at[s, d], at_x(right if d == 0 else left))

    def g_pass(s, d):
        x = left if d == 0 else right
        part = w.gfull.at[s, pl.ds(d * (B // 2), B // 2), pl.ds(shard_rows(x), Q)]
        return rcopy(part, part, w.s_G2.at[s, d], w.r_G2.at[s, d], at_x(right if d == 0 else left))

    def pass_on(first, onward, *s):
        for d in (0, 1):
            first(*s, d).wait_recv()
            onward(*s, d).start()

    up, down = lax.rem(me_y + 1, c.NY), lax.rem(me_y + c.NY - 1, c.NY)

    def b_copy(part, name, k, dev):
        sems = getattr(w, "s_" + name), getattr(w, "r_" + name)
        return rcopy(part, part, sems[0].at[k], sems[1].at[k], dev)

    def bx_first(d):
        return b_copy(w.zb.at[me_g, t], "X1", d, at_x(right if d == 0 else left))

    def bx_pass(d):
        part = w.zb.at[me_g, left if d == 0 else right, pl.ds(d * (NZ // 2), NZ // 2)]
        return b_copy(part, "X2", d, at_x(right if d == 0 else left))

    def at_y(y):
        return at_g(y * c.NC + me_c)

    def by_first(d):
        return b_copy(w.zb.at[me_g], "Y1", d, at_y(up if d == 0 else down))

    def by_pass(d):
        part = w.zb.at[(down if d == 0 else up) * c.NC + me_c, pl.ds(d * (NX // 2), NX // 2)]
        return b_copy(part, "Y2", d, at_y(up if d == 0 else down))

    def b_core(k):
        y = lax.rem(me_y + k, c.NY)
        return b_copy(w.zb.at[y * c.NC + me_c], "K", k, at_g(me_y * c.NC + (1 - me_c)))

    def b_core_in(k):
        y = lax.rem(me_y + k, c.NY)
        return b_copy(w.zb.at[y * c.NC + (1 - me_c)], "K", k, at_g(me_y * c.NC + (1 - me_c)))

    barrier = pltpu.get_barrier_semaphore()

    def greet(at):
        def go(p):
            pl.semaphore_signal(barrier, inc=1, device_id=at(p), device_id_type=MESH)
        return go
    each_z(greet(at_z))
    each_g(greet(at_g))
    each_x(greet(at_x))

    def local(src, dst, sem):
        return pltpu.make_async_copy(src, dst, sem)

    loads = {
        "lr": local(lr, w.lfull.at[:, pl.ds(shard_rows(t), Q), :], w.l_lr.at[0]),
        "rv": local(rr, w.rv, w.l_rv.at[0]),
        "lf": local(lf, w.lfv, w.l_lf.at[0]),
        "rf": local(rf, w.rfv, w.l_rf.at[0]),
    }

    inputs[0].wait()
    spread = hot(imod(iota((c.NBC, NB), 1), c.NBC) == iota((c.NBC, NB), 0))
    wide = dot(owner[...].astype(F32).astype(BF), spread)
    own_row = jnp.sum(
        jnp.where(idiv(iota((c.NBR, NB), 1), c.NBC) == iota((c.NBR, NB), 0), wide, 0.0), axis=0, keepdims=True
    )
    i0, i1 = iota((NB, NB), 0), iota((NB, NB), 1)
    own_col = jnp.sum(jnp.where(i0 == i1, own_row, 0.0), axis=1, keepdims=True)
    same = own_row == own_col
    rank_row = jnp.sum(jnp.where(same & (i0 < i1), 1.0, 0.0), axis=0, keepdims=True).astype(I32)
    rank_col = jnp.sum(jnp.where(same & (i1 < i0), 1.0, 0.0), axis=1, keepdims=True).astype(I32)
    own_row, own_col = own_row.astype(I32), own_col.astype(I32)
    key_row, key_col = own_row * 8 + rank_row, own_col * 8 + rank_col
    z_row, z_col = imod(idiv(own_row, c.NC), NZ), imod(idiv(own_col, c.NC), NZ)

    def key_of(z, g, s):
        return ((idiv(g, c.NC) * NZ + z) * c.NC + imod(g, c.NC)) * 8 + s

    def key_main(m):
        return key_of(idiv(m, MAIN * NG), imod(m, NG), imod(idiv(m, NG), MAIN))

    places = NZ * MAIN * NG
    sel_main = hot(key_main(iota((places, 1), 0)) == key_row)
    inputs[1].wait()
    for r in range(R):
        block = grads[:, r, :, :].reshape(NB, Q)
        w.sA[:, :, r * Q:(r + 1) * Q] = dot(sel_main, block).astype(BF).reshape(NZ, MAIN * NG, Q)

    pl.semaphore_wait(barrier, NZ - 1 + NG - 1 + NX - 1)
    xA.start()
    for s in range(MAIN):
        for d in (0, 1):
            l_first(s, d).start()

    over_row, over_col = rank_row >= MAIN, rank_col >= MAIN
    mates = (z_row == z_col)
    pos_row = jnp.sum(jnp.where(mates & over_col & (i0 < i1), 1.0, 0.0), axis=0, keepdims=True).astype(I32)
    pos_col = jnp.sum(jnp.where(mates & over_row & (i1 < i0), 1.0, 0.0), axis=1, keepdims=True).astype(I32)
    PB = NZ * R * CB
    left_out[0] = jnp.sum(jnp.where(over_row & (pos_row >= CB), 1, 0))
    rest_row = jnp.where(over_row & (pos_row < CB), z_row * CB + pos_row, -1)
    rest_col = jnp.where(over_col & (pos_col < CB), z_col * CB + pos_col, -1)

    def rest_parts(m):
        return idiv(m, R * CB), imod(idiv(m, CB), R), imod(m, CB)

    mz, mr, mb = rest_parts(iota((PB, 1), 0))
    lz, lrr, lb = rest_parts(iota((1, PB), 1))
    m_rest, l_rest = mz * CB + mb, lz * CB + lb
    total = jnp.zeros((PB, Q), F32)
    for r in range(R):
        sel = hot(jnp.where(mr == r, m_rest, -2) == rest_row)
        total += dot(sel, grads[:, r, :, :].reshape(NB, Q))
    w.sB[...] = total.astype(BF).reshape(NZ, R * CB, Q)
    xB.start()
    w.rA[pl.ds(me_z, 1)] = w.sA[pl.ds(me_z, 1)]
    w.zb[pl.ds(me_g, 1), pl.ds(t, 1), pl.ds(me_z, 1)] = w.sB[pl.ds(me_z, 1)][None, None]
    for copy in loads.values():
        copy.start()

    inputs[2].wait()
    adam_col = jnp.zeros((NB, 1), F32)
    for r in range(R):
        g = grads[:, r, :, :].astype(F32)
        moment = 0.95 * sm[:, r, :, :].astype(F32) + 0.05 * g * g
        mom[:, r, :, :] = moment.astype(BF)
        adam = g / (jnp.sqrt(moment) + 1e-08)
        adam_col += jnp.sum((adam * adam).reshape(NB, Q), axis=1, keepdims=True)
    outputs[0].start()
    lane = iota((1, LANES), 1)
    lane_key = jnp.where(lane < NG * 8, key_of(jnp.zeros_like(lane), idiv(lane, 8), imod(lane, 8)), -1)

    def sums_for(z):
        hit = (key_col - z * (c.NC * 8)) == lane_key
        w.az[pl.ds(z, 1)] = jnp.sum(jnp.where(hit, adam_col, 0.0), axis=0, keepdims=True)[None]
    loop(0, NZ, sums_for)
    xz.start()
    w.azr[pl.ds(me_z, 1)] = w.az[pl.ds(me_z, 1)]

    def natural(m):
        r, g, z = idiv(m, NG * NZ), imod(idiv(m, NZ), NG), imod(m, NZ)
        return ((idiv(g, c.NC) * NZ + z) * c.NC + imod(g, c.NC)) * R + r
    w.pi[...] = hot(iota((B, B), 0) == natural(iota((1, B), 1)))
    w.pit[...] = hot(natural(iota((B, 1), 0)) == iota((B, B), 1))

    def turned(m):
        return (imod(m, NZ) * MAIN + imod(idiv(m, NZ), MAIN)) * NG + idiv(m, NZ * MAIN)
    to_gsz = hot(turned(iota((places, 1), 0)) == iota((places, places), 1))
    to_zsg = hot(iota((places, places), 0) == turned(iota((1, places), 1)))

    gm = iota((1, c.NC * PB), 1)
    gc = idiv(gm, PB)
    gz, gr, gb = rest_parts(gm - gc * PB)
    held_row = jnp.sum(
        jnp.where(rest_col == me_z * CB + gb, key_col + 1, 0), axis=0, keepdims=True
    ) - 1
    held_col = jnp.sum(
        jnp.where(me_z * CB + mb == rest_row, key_row + 1, 0), axis=1, keepdims=True
    ) - 1

    def rest_slots(m):
        return idiv(m, REST * NZ), imod(idiv(m, NZ), REST) + MAIN, imod(m, NZ)
    PS = NG * REST * NZ
    bg_, bs_, bz_ = rest_slots(iota((1, PS), 1))
    slot_row = key_of(me_z, bg_, bs_)

    per_y = c.B // c.NY
    n = iota((REST * per_y, 1), 0)
    slot = idiv(n, per_y)
    n = n - slot * per_y
    n_z, n_c, n_r = idiv(n, c.NC * R), imod(idiv(n, R), c.NC), imod(n, R)
    wanted = key_of(me_z, me_g, slot + MAIN)
    w.pick[...] = hot((held_row == wanted) & (gz == n_z) & (gc == n_c) & (gr == n_r))
    for s in range(MAIN):
        pass_on(l_first, l_pass, s)

    for s in range(MAIN, CAP):
        for d in (0, 1):
            l_first(s, d).start()
    xA.recv()
    w.sC[...] = dot(to_gsz, w.rA[...].reshape(places, W)).astype(BF).reshape(NG, MAIN, NZ, W)
    xC.start()
    w.rC[pl.ds(me_g, 1)] = w.sC[pl.ds(me_g, 1)]

    xB.recv()
    for d in (0, 1):
        bx_first(d).start()

    xC.recv()
    for s in range(MAIN):
        rows = [w.rC[:, s, :, r * Q:(r + 1) * Q].reshape(NG * NZ, Q) for r in range(R)]
        cols = dot(w.pi[...], jnp.concatenate(rows, axis=0)).astype(BF)
        w.gown[s] = cols
        w.gfull[s, :, pl.ds(shard_rows(t), Q)] = cols
    pass_on(bx_first, bx_pass)
    for s in range(MAIN):
        for d in (0, 1):
            g_first(s, d).start()

    for d in (0, 1):
        bx_pass(d).wait_recv()
    for d in (0, 1):
        by_first(d).start()
    b_core(0).start()

    for s in range(MAIN):
        pass_on(g_first, g_pass, s)

    for s in range(MAIN, CAP):
        pass_on(l_first, l_pass, s)

    pass_on(by_first, by_pass)
    b_core(1).start()
    b_core(c.NY - 1).start()

    loads["lr"].wait()
    loads["rv"].wait()
    norm_row = jnp.zeros((1, LANES), F32)

    def precond(s, dest, at):
        for d in (0, 1):
            l_pass(s, d).wait_recv()
            if s < MAIN:
                g_pass(s, d).wait_recv()
        cols = dot(w.gfull[s], w.rv[s])
        high = cols.astype(BF)
        low = (cols - high.astype(F32)).astype(BF)
        out = (dot(w.lfull[s], high) + dot(w.lfull[s], low)).astype(BF)
        moved = dot(w.pit[...], out).astype(BF)
        for r in range(R):
            dest[:, at, :, r * Q:(r + 1) * Q] = moved[r * NG * NZ:(r + 1) * NG * NZ].reshape(NG, NZ, Q)
        wide_out = out.astype(F32)
        total = jnp.sum(jnp.sum(wide_out * wide_out, axis=0, keepdims=True), axis=1, keepdims=True)
        return jnp.where(lane == s, total, norm_row)

    for s in range(MAIN):
        norm_row = precond(s, w.sF, s)
    xF.start()
    w.rF[pl.ds(me_g, 1)] = w.sF[pl.ds(me_g, 1)]

    for d in (0, 1):
        by_pass(d).wait_recv()
    b_core(2).start()

    xz.recv()
    w.ag[...] = jnp.sum(w.azr[...], axis=0, keepdims=True)
    xg.start()
    w.agr[pl.ds(me_g, 1)] = w.ag[...]

    for k in range(c.NY):
        b_core_in(k).wait_recv()

    def place(y):
        parts = [
            jnp.concatenate([w.zb[y * c.NC + k, x].reshape(PB, Q) for x in range(NX)], axis=1)
            for k in range(c.NC)
        ]
        got = dot(w.pick[...], jnp.concatenate(parts, axis=0)).astype(BF)
        for k in range(REST):
            rows = pl.ds(pl.multiple_of(y * per_y, per_y), per_y)
            w.gfull[MAIN + k, rows, :] = got[k * per_y:(k + 1) * per_y]
    loop(0, c.NY, place)

    xF.recv()
    w.sI[...] = dot(to_zsg, w.rF[...].reshape(places, W)).astype(BF).reshape(NZ, MAIN * NG, W)
    xI.start()
    w.rI[pl.ds(me_z, 1)] = w.sI[pl.ds(me_z, 1)]

    for s in range(MAIN, CAP):
        norm_row = precond(s, w.sH, s - MAIN)
    xH.start()
    w.rH[pl.ds(me_g, 1)] = w.sH[pl.ds(me_g, 1)]
    w.pa[...] = norm_row[None]
    xpa.start()
    w.par[pl.ds(t, 1)] = w.pa[...]

    xg.recv()
    w.ax[...] = jnp.sum(w.agr[...], axis=0, keepdims=True)
    xx.start()
    w.axr[pl.ds(t, 1)] = w.ax[...]
    loads["lf"].wait()
    loads["rf"].wait()

    def factor(s):
        rows = w.gfull[s, pl.ds(shard_rows(t), Q), :]
        gram = lax.dot_general(rows, w.gfull[s], (((1,), (1,)), ((), ())), preferred_element_type=F32)
        w.lnv[s] = (0.9 * w.lfv[s].astype(F32) + 0.1 * gram).astype(BF)
        cols = w.gfull[s, :, pl.ds(shard_rows(t), Q)]
        gram = lax.dot_general(cols, w.gfull[s], (((0,), (0,)), ((), ())), preferred_element_type=F32)
        w.rnv[s] = (0.9 * w.rfv[s].astype(F32) + 0.1 * gram).astype(BF)

    for s in range(MAIN):
        factor(s)

    xx.recv()
    xpa.recv()
    adam_all = jnp.sum(w.axr[...], axis=0)
    norm_all = jnp.sum(w.par[...], axis=0)
    scales = jnp.zeros((1, LANES), F32)
    for s in range(CAP):
        adam_sum = jnp.sum(jnp.where(lane == me_g * 8 + s, adam_all, 0.0), axis=1, keepdims=True)
        norm_sum = jnp.sum(jnp.where(lane == s, norm_all, 0.0), axis=1, keepdims=True)
        scale = jnp.sqrt(adam_sum) / (jnp.sqrt(norm_sum) + 1e-06)
        scales = jnp.where(lane == me_g * 8 + s, scale, scales)
    w.wg[...] = scales[None]
    xwg.start()
    w.wgr[pl.ds(me_g, 1)] = w.wg[...]

    hits = (held_col == slot_row) & (mz == bz_)
    sel_rest = [hot(hits & (mr == r)) for r in range(R)]
    xH.recv()
    flat = [w.rH[:, :, :, r * Q:(r + 1) * Q].reshape(PS, Q) for r in range(R)]
    total = jnp.zeros((PB, Q), F32)
    for r in range(R):
        total += dot(sel_rest[r], flat[r])
    w.sJ[...] = total.astype(BF).reshape(NZ, R * CB, Q)
    xJ.start()
    w.rJ[pl.ds(me_z, 1)] = w.sJ[pl.ds(me_z, 1)]

    xwg.recv()
    w.wz[...] = jnp.sum(w.wgr[...], axis=0, keepdims=True)
    xwz.start()
    w.wzr[pl.ds(me_z, 1)] = w.wz[...]

    for s in range(MAIN, CAP):
        factor(s)
    factors = (local(w.lnv, ln, w.l_ln.at[0]), local(w.rnv, rn, w.l_rn.at[0]))
    for copy in factors:
        copy.start()

    sel_back = hot(key_col == key_main(iota((1, places), 1)))
    rest_back = [hot(rest_col == jnp.where(lrr == r, l_rest, -2)) for r in range(R)]
    xI.recv()
    main_part = [dot(sel_back, w.rI[:, :, r * Q:(r + 1) * Q].reshape(places, Q)) for r in range(R)]
    xwz.recv()

    def scale_of(z, total):
        return total + jnp.where((key_col - z * (c.NC * 8)) == lane_key, w.wzr[z], 0.0)
    scale_col = jnp.sum(
        lax.fori_loop(0, NZ, scale_of, jnp.zeros((NB, LANES), F32)), axis=1, keepdims=True
    )
    xJ.recv()
    rest = w.rJ[...].reshape(PB, Q)
    for r in range(R):
        out = main_part[r] + dot(rest_back[r], rest)
        upd[:, r, :, :] = (out * scale_col).astype(BF).reshape(c.NBR, c.NBC, Q)

    outputs[1].start()
    for copy in outputs:
        copy.wait()
    for x in (xA, xB, xz, xC, xg, xx, xpa, xF, xH, xI, xJ, xwg, xwz):
        x.sent()
    for d in (0, 1):
        for copy in (bx_first(d), bx_pass(d), by_first(d), by_pass(d)):
            copy.wait_send()
        for s in range(CAP):
            l_first(s, d).wait_send()
            l_pass(s, d).wait_send()
        for s in range(MAIN):
            g_first(s, d).wait_send()
            g_pass(s, d).wait_send()
    for k in range(c.NY):
        b_core(k).wait_send()
    for copy in factors:
        copy.wait()


def finish(results):
    count = len(results)

    def body(*refs):
        ins, outs, held, (got, put) = refs[:count], refs[count:2 * count], refs[2 * count:3 * count], refs[3 * count:]
        arrays = list(enumerate(zip(ins, held, outs)))
        for k, (a, v, _) in arrays:
            pltpu.make_async_copy(a, v, got.at[k]).start()
        for k, (a, v, o) in arrays:
            pltpu.make_async_copy(a, v, got.at[k]).wait()
            pltpu.make_async_copy(v, o, put.at[k]).start()
        for k, (_, v, o) in arrays:
            pltpu.make_async_copy(v, o, put.at[k]).wait()
    hbm = pl.BlockSpec(memory_space=pltpu.HBM)
    return tuple(pl.pallas_call(
        body,
        out_shape=tuple(jax.ShapeDtypeStruct(a.shape, a.dtype) for a in results),
        in_specs=[hbm] * count,
        out_specs=(hbm,) * count,
        scratch_shapes=[pltpu.VMEM(a.shape, a.dtype) for a in results] + [pltpu.SemaphoreType.DMA((count,))] * 2,
        compiler_params=pltpu.CompilerParams(vmem_limit_bytes=VMEM_BYTES),
        name="finish",
    )(*results))


def step(c, grads, second_moment, owner, left_factor, right_factor, left_root, right_root):
    scratch = scratch_of(c)
    vmem, hbm = pl.BlockSpec(memory_space=pltpu.VMEM), pl.BlockSpec(memory_space=pltpu.HBM)
    smem = pl.BlockSpec(memory_space=pltpu.SMEM)
    like = lambda a: jax.ShapeDtypeStruct(a.shape, a.dtype)
    return pl.pallas_call(
        functools.partial(kernel, c, tuple(scratch)),
        out_shape=(
            like(grads), like(second_moment), like(left_factor), like(right_factor),
            jax.ShapeDtypeStruct((1,), I32),
        ),
        in_specs=[hbm] * 7,
        out_specs=(hbm, hbm, hbm, hbm, smem),
        scratch_shapes=list(scratch.values()),
        compiler_params=pltpu.CompilerParams(
            collective_id=c.cid, has_side_effects=True, vmem_limit_bytes=VMEM_BYTES
        ),
        name="shampoo",
    )(grads, second_moment, owner, left_factor, right_factor, left_root, right_root)


def per_device(few, enough, *args):
    *results, left_out = step(few, *args)
    return lax.cond(
        left_out[0] == 0,
        lambda: finish(results),
        lambda: finish(step(enough, *args)[:4]),
    )


def build(mesh, body):
    rows, cols = P(None, "fsdp", None, "tp"), P("fsdp", "tp", None)
    return jax.shard_map(
        body, mesh=mesh,
        in_specs=(rows, rows, P(), cols, cols, cols, P("fsdp", None, "tp")),
        out_specs=(rows, rows, cols, cols), check_vma=False,
    )


def solution(mesh):
    few = cfg_of(4, 16, 2, 4, 4, 128, 16, 16, 4, 1)
    enough = cfg_of(4, 16, 2, 4, 4, 128, 16, 16, 24, 2)
    return build(mesh, functools.partial(per_device, few, enough))
```
